256 devices in a mesh: op: 32 (over x, y, core), sec: 8 (over z).
Axes of the slice: x: 4, y: 4, z: 8, core: 2. Of those that a mesh axis runs over, the one named last changes fastest.
Arguments:
- wavefunction: bfloat16 [8192, 128], P(('op', 'sec')), may hold values from -6 to 6
- left_ops: bfloat16 [16384, 128, 128], P(('op', 'sec')), may hold values from -0.5 to 0.5
- right_ops: bfloat16 [16384, 128, 128], P(('op', 'sec')), may hold values from -0.0078125 to 0.0078125
- davidson_basis: bfloat16 [4, 64, 128, 128], P(None, 'sec'), may hold values from -0.005859375 to 0.005859375
- term_left: int32 [262144], P(('op', 'sec')), may hold values from 0 to 63
- term_right: int32 [262144], P(('op', 'sec')), may hold values from 0 to 63
- term_source: int32 [262144], P(('op', 'sec')), may hold values from 0 to 63
- term_target: int32 [262144], P(('op', 'sec')), may hold values from 0 to 7
- term_count: int32 [256], P(('op', 'sec')), may hold values from 256 to 1024, as said below
Outputs:
- sigma_blocks: float32 [64, 128, 128], P('sec')
- correlations: float32 [4], replicated
The draws below stay inside these ranges and needn't reach their ends.
Inputs may be any that keep to these rules, and one draw needn't show every extreme that they name: `term_count`: some device has all 1024 slots live and some device has 256 live.
All inputs are finite; a program needn't handle non-finite values.
Results may differ from the reference program's by a relative error of at most 0.004.
Values may be sent and summed in bfloat16 or wider, within the bound.
A program may use at most 128 MiB of HBM per device.

```python
import jax
import jax.numpy as jnp
from jax import lax

B = 128
SEC_DEV = 8
TERM_DEV = 1024
OPS_DEV = 64
K = 4
TERM_BLOCK = 128
NODES = 256
S = 64
ROWS = 8192
OPS = 16384
TERMS = 262144
N_OP = 32
N_SEC = 8


def draw_term_count(key, part):
    key = jax.random.fold_in(key, 7)
    keys = jax.random.split(key, 3)
    counts = jax.random.randint(keys[0], (NODES,), TERM_DEV // 4, TERM_DEV + 1, dtype=jnp.int32)
    top_slot = jax.random.randint(keys[1], (), 0, NODES, dtype=jnp.int32)
    low_step = jax.random.randint(keys[2], (), 1, NODES, dtype=jnp.int32)
    low_slot = (top_slot + low_step) % NODES
    counts = counts.at[top_slot].set(TERM_DEV)
    counts = counts.at[low_slot].set(TERM_DEV // 4)
    return counts


def with_ends(result, rng, least, largest):
    extent = result.shape
    spot = [jax.random.randint(jax.random.fold_in(rng, axis), (), 0, extent[axis]) for axis in range(len(extent))]
    result = result.at[tuple(spot)].set(least)
    longest = extent.index(max(extent))
    spot[longest] = (spot[longest] + 1) % extent[longest]
    return result.at[tuple(spot)].set(largest)


def block_levels(rng, shape, pieces, smallest, largest):
    factor_of, own = 1.0, jax.random.fold_in(rng, 6)
    for axis_at, blocks in pieces:
        heights = jnp.exp(jax.random.uniform(jax.random.fold_in(own, axis_at), (blocks,), jnp.float32, smallest / len(pieces), largest / len(pieces)))
        factor_of = factor_of * jnp.repeat(heights, shape[axis_at] // blocks).reshape([-1 if axis == axis_at else 1 for axis in range(len(shape))])
    return factor_of


def gaussian(key, extent, scale, limit, cuts=(), kind=jnp.bfloat16):
    drawn = scale * jax.random.normal(key, extent, jnp.float32)
    if cuts:
        drawn = drawn * block_levels(key, extent, cuts, -0.22, 0.18)
    return jnp.clip(drawn, -limit, limit).astype(kind)


def setup_inputs(seed: int = 0) -> dict:
    seeds = jax.random.split(jax.random.key(seed), 10)
    wavefunction = gaussian(seeds[0], (ROWS, B), 1.0, 6.0, ((0, 256),))
    left_ops = gaussian(seeds[1], (OPS, B, B), B ** -0.5, 0.5, ((0, 256),))
    right_ops = gaussian(seeds[2], (OPS, B, B), (B * TERM_DEV * N_OP // SEC_DEV) ** -0.5, 0.0078125, ((0, 256),))
    davidson_basis = gaussian(seeds[3], (K, S, B, B), (S * B * B) ** -0.5, 0.005859375, ((1, 8),))
    term_left = with_ends(jax.random.randint(seeds[4], (TERMS,), 0, OPS_DEV), jax.random.fold_in(seeds[4], 1), 0, OPS_DEV - 1).astype(jnp.int32)
    term_right = with_ends(jax.random.randint(seeds[5], (TERMS,), 0, OPS_DEV), jax.random.fold_in(seeds[5], 1), 0, OPS_DEV - 1).astype(jnp.int32)
    term_source = with_ends(jax.random.randint(seeds[6], (TERMS,), 0, S), jax.random.fold_in(seeds[6], 1), 0, S - 1).astype(jnp.int32)
    term_target = with_ends(jax.random.randint(seeds[7], (TERMS,), 0, SEC_DEV), jax.random.fold_in(seeds[7], 1), 0, SEC_DEV - 1).astype(jnp.int32)
    term_count = draw_term_count(jax.random.fold_in(seeds[9], 71), 0)
    return dict(wavefunction=wavefunction, left_ops=left_ops, right_ops=right_ops, davidson_basis=davidson_basis, term_left=term_left, term_right=term_right, term_source=term_source, term_target=term_target, term_count=term_count)


def reference(wavefunction, left_ops, right_ops, davidson_basis, term_left, term_right, term_source, term_target, term_count):
    blocks = wavefunction.reshape(S, B, B)
    upper_limit = lax.Precision.HIGHEST

    def add_block(sigma_acc, block_id):
        first_term = (block_id * TERM_BLOCK).astype(jnp.int32)
        term_index = first_term + jnp.arange(TERM_BLOCK, dtype=jnp.int32)
        owners = term_index // TERM_DEV
        is_live = (term_index % TERM_DEV) < term_count[owners]
        left_operator_index = lax.dynamic_slice_in_dim(term_left, first_term, TERM_BLOCK)
        right_index = lax.dynamic_slice_in_dim(term_right, first_term, TERM_BLOCK)
        source_index = lax.dynamic_slice_in_dim(term_source, first_term, TERM_BLOCK)
        target_index = lax.dynamic_slice_in_dim(term_target, first_term, TERM_BLOCK)
        left_environment_blocks = left_ops[owners * OPS_DEV + left_operator_index].astype(jnp.float32)
        right_environment_blocks = right_ops[owners * OPS_DEV + right_index].astype(jnp.float32)
        source_sectors = blocks[source_index].astype(jnp.float32)
        half_product = jnp.einsum('esg,egu->esu', left_environment_blocks, source_sectors, precision=upper_limit).astype(jnp.bfloat16)
        half_product = lax.optimization_barrier(half_product).astype(jnp.float32)
        term_products = jnp.einsum('wfi,woi->wfo', half_product, right_environment_blocks, precision=upper_limit)
        term_products = term_products * is_live.astype(jnp.float32)[:, None, None]
        targets = (owners % N_SEC) * SEC_DEV + target_index
        return sigma_acc.at[targets].add(term_products), None

    empty_acc = jnp.zeros((S, B, B), jnp.float32)
    sigma_blocks, _ = lax.scan(add_block, empty_acc, jnp.arange(TERMS // TERM_BLOCK, dtype=jnp.int32))
    correlations = jnp.einsum('ksab,sab->k', davidson_basis.astype(jnp.float32), sigma_blocks, precision=upper_limit)
    return sigma_blocks, correlations
```

```python
import functools

import jax
import jax.numpy as jnp
from jax import lax
from jax.experimental import pallas as pl
from jax.experimental.pallas import tpu as pltpu
from jax.sharding import PartitionSpec as P

MESH = pl.DeviceIdType.MESH
BF, F32, I32 = jnp.bfloat16, jnp.float32, jnp.int32
SLOTS = 1024
CHUNK = 8
CHUNKS = 136
NT = (((1,), (1,)), ((), ()))


def remote(src, dst, send_sem, recv_sem, to):
    return pltpu.make_async_remote_copy(
        src_ref=src,
        dst_ref=dst,
        send_sem=send_sem,
        recv_sem=recv_sem,
        device_id=to,
        device_id_type=MESH,
    )


def fold(mask_or_value):
    return jnp.sum(mask_or_value.reshape(16, 8, 128), axis=0)


def sort_terms(tl, tr, ts, tt, count):
    row = lax.broadcasted_iota(I32, (8, 128), 0)
    lane = lax.broadcasted_iota(I32, (8, 128), 1)
    slot = row * 128 + lane
    live = slot < count
    rank_key = jnp.where(live, tt, 8) * SLOTS + slot
    value = (slot + 1) | (tr << 11)
    key_t, value_t = rank_key.T, value.T
    ranks = [jnp.zeros((8, 128), I32) for _ in range(8)]
    for j in range(8):
        key_j = jnp.broadcast_to(key_t[:, j : j + 1], (128, 128))
        for i in range(8):
            ranks[i] = ranks[i] + fold((key_j < rank_key[i : i + 1, :]).astype(I32))
    rank = jnp.concatenate([jnp.sum(r, axis=0, keepdims=True) for r in ranks], axis=0)
    base = jnp.zeros((1, 1), I32)
    start = jnp.zeros((1, 1), I32)
    place = jnp.where(live, rank, 1 << 20)
    restart = jnp.zeros((8, 128), I32)
    last = jnp.full((8, 128), CHUNKS, I32)
    for t in range(8):
        hit = live & (tt == t)
        n = jnp.sum(jnp.sum(hit.astype(I32), axis=0, keepdims=True), axis=1, keepdims=True)
        place = place + jnp.where(hit, start - base, 0)
        restart = restart | ((start == slot * CHUNK) & (n > 0)).astype(I32)
        base = base + n
        start = start + (((n + CHUNK - 1) >> 3) << 3)
        last = jnp.where((lane == t) & (n > 0), (start >> 3) - 1, last)
    place_t = place.T
    tables = [jnp.zeros((8, 128), I32) for _ in range(9)]
    for j in range(8):
        place_j = jnp.broadcast_to(place_t[:, j : j + 1], (128, 128))
        value_j = jnp.broadcast_to(value_t[:, j : j + 1], (128, 128))
        for i in range(9):
            at = lax.broadcasted_iota(I32, (128, 128), 1) + i * 128
            tables[i] = tables[i] + fold(jnp.where(place_j == at, value_j, 0))
    tables = [jnp.sum(t, axis=0, keepdims=True) for t in tables]
    tail = jnp.concatenate([tables[8], jnp.zeros((7, 128), I32)], axis=0)
    ends = jnp.where(row < 2, 1 - restart, last)
    return tl | (ts << 6), jnp.concatenate(tables[:8], axis=0), tail, ends


def kernel(
    w_ref,
    left_hbm,
    right_hbm,
    basis_hbm,
    tl_ref,
    tr_ref,
    ts_ref,
    tt_ref,
    count_ref,
    sigma_ref,
    corr_ref,
    xb,
    left,
    right,
    basis,
    half,
    sums,
    tab_v,
    tab_s,
    sig,
    part,
    inbox,
    outbox,
    corr_z,
    corr_p,
    local_sem,
    ag_send,
    ag_recv,
    rs_send,
    rs_recv,
    out_send,
    out_recv,
    cz_send,
    cz_recv,
    cp_send,
    cp_recv,
):
    op = lax.axis_index("op")
    z = lax.axis_index("sec")
    x, y, c = op // 8, (op // 2) % 4, op % 2

    def at(xx, yy, cc, zz):
        return {"op": (xx * 4 + yy) * 2 + cc, "sec": zz}

    z_peers = [at(x, y, c, (z + k) % 8) for k in range(1, 8)]
    y_peers = [at(x, (y + k) % 4, c, z) for k in range(1, 4)]
    x_peers = [at((x + k) % 4, y, c, z) for k in range(1, 4)]
    plane = [{"op": (op + k) % 32, "sec": z} for k in range(1, 32)]
    twin = at(x, y, 1 - c, z)

    barrier = pltpu.get_barrier_semaphore()
    for peer in z_peers + plane:
        pl.semaphore_signal(barrier, inc=1, device_id=peer, device_id_type=MESH)

    mine = xb.at[x, y, 2 * c + z // 4, pl.ds(pl.multiple_of((z % 4) * 32, 32), 32)]
    loads = [
        pltpu.make_async_copy(w_ref, mine, local_sem.at[0]),
        pltpu.make_async_copy(right_hbm, right, local_sem.at[1]),
        pltpu.make_async_copy(left_hbm, left, local_sem.at[2]),
        pltpu.make_async_copy(basis_hbm, basis, local_sem.at[3]),
    ]
    for load in loads:
        load.start()
    tables = sort_terms(tl_ref[...], tr_ref[...], ts_ref[...], tt_ref[...], count_ref[0])
    for i, table in enumerate(tables):
        tab_v[i] = table
    to_smem = pltpu.make_async_copy(tab_v, tab_s, local_sem.at[4])
    to_smem.start()
    half[0] = jnp.zeros((128, 128), BF)
    sums[CHUNKS] = jnp.zeros((128, 128), F32)
    to_smem.wait()
    for load in loads:
        load.wait()
    pl.semaphore_wait(barrier, 38)

    copies = []

    def push(src, to):
        i = len(copies)
        copy = remote(src, src, ag_send.at[i], ag_recv.at[i], to)
        copy.start()
        copies.append(copy)
        return copy

    first = [push(mine, peer) for peer in z_peers]
    for copy in first:
        copy.wait_recv()
    lo, hi = xb.at[x, y, 2 * c], xb.at[x, y, 2 * c + 1]
    along_y = [push(lo, peer) for peer in y_peers]
    along_x = [push(hi, peer) for peer in x_peers]
    relayed = [push(xb.at[x, y, pl.ds(2 * c, 2)], twin)]
    for copy in along_y + along_x:
        copy.wait_recv()
    row, column = xb.at[x, :, 2 * c], xb.at[:, y, 2 * c + 1]
    rows = [push(row, peer) for peer in x_peers]
    columns = [push(column, peer) for peer in y_peers]
    for k in range(1, 4):
        relayed.append(push(xb.at[x, (y + k) % 4, 2 * c], twin))
        relayed.append(push(xb.at[(x + k) % 4, y, 2 * c + 1], twin))
    for k in (0, 2, 1):
        rows[k].wait_recv()
        relayed.append(push(xb.at[(x + 3 - k) % 4, :, 2 * c], twin))
        columns[k].wait_recv()
        relayed.append(push(xb.at[:, (y + 3 - k) % 4, 2 * c + 1], twin))
    for copy in relayed:
        copy.wait_recv()

    def products(i, carry):
        for u in range(128):
            word = tab_s[0, i, u]
            l, s = word & 63, (word >> 6) & 63
            block = xb[s >> 4, (s >> 2) & 3, s & 3]
            half[i * 128 + u + 1] = jnp.dot(left[l], block, preferred_element_type=F32).astype(BF)
        return carry

    lax.fori_loop(0, SLOTS // 128, products, 0)

    def chunk_sums(i, acc):
        for v in range(17):
            chunk = i * 17 + v
            words = []
            for k in range(CHUNK):
                slot = chunk * CHUNK + k
                words.append(tab_s[1 + (slot >> 10), (slot >> 7) & 7, slot & 127])
            halves = jnp.concatenate([half[w & 2047] for w in words], axis=1)
            rights = jnp.concatenate([right[w >> 11] for w in words], axis=1)
            prod = lax.dot_general(halves, rights, NT, preferred_element_type=F32)
            keep = tab_s[3, chunk >> 7, chunk & 127]
            acc = acc * keep.astype(F32) + prod
            sums[chunk] = acc
        return acc

    lax.fori_loop(0, CHUNKS // 17, chunk_sums, jnp.zeros((128, 128), F32))

    def targets(p, carry):
        for h in range(2):
            total = sums[tab_s[3, 2, 2 * p + h]]
            sig[2 * p + h] = total
            part[p, 4 * h : 4 * h + 4] = total.astype(BF).reshape(4, 32, 128)
        for k in range(8):
            xo, co = (x + k // 2) % 4, (c + k) % 2
            yo = (p - xo + 4) % 4
            owner = (xo * 4 + yo) * 2 + co
            index = (op - owner + 31) % 32
            copy = remote(
                part.at[p, xo * 2 + co],
                inbox.at[index],
                rs_send,
                rs_recv,
                {"op": owner, "sec": z},
            )
            if k == 0:
                pl.when(owner != op)(copy.start)
            else:
                copy.start()
        return carry

    lax.fori_loop(0, 4, targets, 0)

    inner_sums = []
    for k in range(4):
        def inner(b, acc, k=k):
            prod = basis[k, b].astype(F32) * sig[b]
            return acc + jnp.sum(prod.reshape(16, 8, 128), axis=0)

        total = lax.fori_loop(0, 8, inner, jnp.zeros((8, 128), F32))
        inner_sums.append(jnp.sum(total, axis=0, keepdims=True))
    corr_z[z] = jnp.concatenate(inner_sums + [jnp.zeros((4, 128), F32)], axis=0)
    to_z = []
    for k, peer in enumerate(z_peers):
        copy = remote(corr_z.at[z], corr_z.at[z], cz_send.at[k], cz_recv.at[k], peer)
        copy.start()
        to_z.append(copy)

    whole = remote(inbox, inbox, rs_send, rs_recv, twin)
    whole.wait_recv()
    p_me, m_me = (x + y) % 4, x * 2 + c
    total = part[p_me, m_me].astype(F32)
    for k in range(31):
        total = total + inbox[k].astype(F32)
    t_me, r_me = 2 * p_me + m_me // 4, pl.multiple_of((m_me % 4) * 32, 32)
    out_mine = outbox.at[t_me, pl.ds(r_me, 32)]
    out_mine[...] = total.astype(BF)
    to_out = []
    for k, peer in enumerate(plane):
        copy = remote(out_mine, out_mine, out_send.at[k], out_recv.at[k], peer)
        copy.start()
        to_out.append(copy)

    for copy in to_z:
        copy.wait_recv()
    z_sum = corr_z[0]
    for k in range(1, 8):
        z_sum = z_sum + corr_z[k]
    corr_p[op] = z_sum
    to_plane = []
    for k, peer in enumerate(plane):
        copy = remote(corr_p.at[op], corr_p.at[op], cp_send.at[k], cp_recv.at[k], peer)
        copy.start()
        to_plane.append(copy)

    for copy in to_out:
        copy.wait_recv()
    sigma_ref[...] = outbox[...]
    for copy in to_plane:
        copy.wait_recv()
    p_sum = corr_p[0]
    for k in range(1, 32):
        p_sum = p_sum + corr_p[k]
    corr_ref[...] = jnp.broadcast_to(jnp.sum(p_sum, axis=1, keepdims=True), (8, 128))

    for copy in copies + to_z + to_out + to_plane:
        copy.wait_send()
    whole.wait_send()


def body(wavefunction, left_ops, right_ops, basis, tl, tr, ts, tt, count):
    vmem = pl.BlockSpec(memory_space=pltpu.VMEM)
    smem = pl.BlockSpec(memory_space=pltpu.SMEM)
    hbm = pl.BlockSpec(memory_space=pl.ANY)
    dma = pltpu.SemaphoreType.DMA
    sigma, corr = pl.pallas_call(
        kernel,
        out_shape=(
            jax.ShapeDtypeStruct((8, 128, 128), BF),
            jax.ShapeDtypeStruct((8, 128), F32),
        ),
        in_specs=[vmem, hbm, hbm, hbm, vmem, vmem, vmem, vmem, smem],
        out_specs=(vmem, vmem),
        scratch_shapes=[
            pltpu.VMEM((4, 4, 4, 128, 128), BF),
            pltpu.VMEM((64, 128, 128), BF),
            pltpu.VMEM((64, 128, 128), BF),
            pltpu.VMEM((4, 8, 128, 128), BF),
            pltpu.VMEM((SLOTS + 1, 128, 128), BF),
            pltpu.VMEM((CHUNKS + 1, 128, 128), F32),
            pltpu.VMEM((4, 8, 128), I32),
            pltpu.SMEM((4, 8, 128), I32),
            pltpu.VMEM((8, 128, 128), F32),
            pltpu.VMEM((4, 8, 32, 128), BF),
            pltpu.VMEM((31, 32, 128), BF),
            pltpu.VMEM((8, 128, 128), BF),
            pltpu.VMEM((8, 8, 128), F32),
            pltpu.VMEM((32, 8, 128), F32),
            dma((5,)),
            dma((32,)),
            dma((32,)),
            dma(()),
            dma(()),
            dma((31,)),
            dma((31,)),
            dma((7,)),
            dma((7,)),
            dma((31,)),
            dma((31,)),
        ],
        compiler_params=pltpu.CompilerParams(
            collective_id=0, has_side_effects=True, vmem_limit_bytes=60 * 1024 * 1024
        ),
    )(
        wavefunction,
        left_ops,
        right_ops,
        basis,
        *(t.reshape(8, 128) for t in (tl, tr, ts, tt)),
        count,
    )
    return sigma.astype(F32), corr[:4, 0]


def solution(mesh):
    placed = (
        P(("op", "sec"), None),
        P(("op", "sec"), None, None),
        P(("op", "sec"), None, None),
        P(None, "sec", None, None),
        P(("op", "sec")),
        P(("op", "sec")),
        P(("op", "sec")),
        P(("op", "sec")),
        P(("op", "sec")),
    )
    return jax.shard_map(
        body, mesh=mesh, in_specs=placed, out_specs=(P("sec", None, None), P()), check_vma=False
    )
```

```python
import functools

import jax
import jax.numpy as jnp
from jax import lax
from jax.experimental import pallas as pl
from jax.experimental.pallas import tpu as pltpu
from jax.sharding import PartitionSpec as P

MESH = pl.DeviceIdType.MESH
BF, F32, I32 = jnp.bfloat16, jnp.float32, jnp.int32
SLOTS = 1024
CHUNK = 8
CHUNKS = 136
STAGED = ((304, 392, 328), (44, 78, 108, 136))
GENERAL = ((0, 0, 1024), (136, 136, 136, 136))
NT = (((1,), (1,)), ((), ()))


def remote(src, dst, send_sem, recv_sem, to):
    return pltpu.make_async_remote_copy(
        src_ref=src,
        dst_ref=dst,
        send_sem=send_sem,
        recv_sem=recv_sem,
        device_id=to,
        device_id_type=MESH,
    )


def fold(mask_or_value):
    return jnp.sum(mask_or_value.reshape(16, 8, 128), axis=0)


def ranks_of(key):
    key_t = key.T
    ranks = [jnp.zeros((8, 128), I32) for _ in range(8)]
    for j in range(8):
        key_j = jnp.broadcast_to(key_t[:, j : j + 1], (128, 128))
        for i in range(8):
            ranks[i] = ranks[i] + fold((key_j < key[i : i + 1, :]).astype(I32))
    return jnp.concatenate([jnp.sum(r, axis=0, keepdims=True) for r in ranks], axis=0)


def scatter(place, value, rows):
    place_t, value_t = place.T, value.T
    tables = [jnp.zeros((8, 128), I32) for _ in range(rows)]
    for j in range(8):
        place_j = jnp.broadcast_to(place_t[:, j : j + 1], (128, 128))
        value_j = jnp.broadcast_to(value_t[:, j : j + 1], (128, 128))
        for i in range(rows):
            at = lax.broadcasted_iota(I32, (128, 128), 1) + i * 128
            tables[i] = tables[i] + fold(jnp.where(place_j == at, value_j, 0))
    return [jnp.sum(t, axis=0, keepdims=True) for t in tables]


def count_of(mask):
    return jnp.sum(jnp.sum(mask.astype(I32), axis=0, keepdims=True), axis=1, keepdims=True)


def sort_terms(tl, tr, ts, tt, count, x, y, plan):
    row = lax.broadcasted_iota(I32, (8, 128), 0)
    lane = lax.broadcasted_iota(I32, (8, 128), 1)
    slot = row * 128 + lane
    live = slot < count

    dx, dy, odd = ((ts >> 4) - x) & 3, ((ts >> 2) - y) & 3, (ts & 1) == 1
    near, far = jnp.where(odd, dx, dy), jnp.where(odd, dy, dx)
    late = jnp.where((far == 0) | (near == 0), 0, 1)
    late = jnp.where(far == 2, 2, late)
    stages, marks = plan
    spot = ranks_of(jnp.where(live, late, 3) * SLOTS + slot)
    done, end = jnp.zeros((1, 1), I32), jnp.zeros((1, 1), I32)
    for i in range(3):
        n = count_of(live & (late == i))
        begin = jnp.maximum(end, sum(stages[:i]))
        spot = spot + jnp.where(late == i, begin - done, 0)
        done, end = done + n, begin + n
    over = jnp.maximum(end - SLOTS, 0)
    spot = jnp.where(live, spot, 1 << 20)
    first = jnp.concatenate(scatter(spot, tl | (ts << 6), 8), axis=0)
    spot = jnp.minimum(spot, SLOTS - 1)

    rank = ranks_of(jnp.where(live, tt, 8) * SLOTS + slot)
    base = jnp.zeros((1, 1), I32)
    start = jnp.zeros((1, 1), I32)
    place = jnp.where(live, rank, 1 << 20)
    restart = jnp.zeros((8, 128), I32)
    last = jnp.full((8, 128), CHUNKS, I32)
    for t in range(8):
        hit = live & (tt == t)
        n = count_of(hit)
        place = place + jnp.where(hit, start - base, 0)
        restart = restart | ((start == slot * CHUNK) & (n > 0)).astype(I32)
        base = base + n
        start = start + (((n + CHUNK - 1) >> 3) << 3)
        last = jnp.where((lane == t) & (n > 0), (start >> 3) - 1, last)
        over = jnp.maximum(over, start - CHUNK * marks[t // 2])
    tables = scatter(place, (spot + 1) | (tr << 11), 9)
    tail = jnp.concatenate([tables[8], jnp.zeros((7, 128), I32)], axis=0)
    ends = jnp.where(row < 2, 1 - restart, last)
    return first, jnp.concatenate(tables[:8], axis=0), tail, ends, over


def kernel(
    plan,
    w_ref,
    left_hbm,
    right_hbm,
    basis_hbm,
    tl_ref,
    tr_ref,
    ts_ref,
    tt_ref,
    count_ref,
    sigma_ref,
    corr_ref,
    over_ref,
    xb1,
    xb2,
    xb3,
    left,
    right,
    basis,
    half,
    sums,
    tab_v,
    tab_s,
    sig,
    part,
    inbox,
    outbox,
    corr_z,
    corr_p,
    local_sem,
    ag_send,
    ag_recv,
    rs_send,
    rs_recv,
    out_send,
    out_recv,
    cz_send,
    cz_recv,
    cp_send,
    cp_recv,
):
    op = lax.axis_index("op")
    z = lax.axis_index("sec")
    x, y, c = op // 8, (op // 2) % 4, op % 2

    def at(xx, yy, cc, zz):
        return {"op": (xx * 4 + yy) * 2 + cc, "sec": zz}

    z_peers = [at(x, y, c, (z + k) % 8) for k in range(1, 8)]
    y_peers = [at(x, (y + k) % 4, c, z) for k in range(1, 4)]
    x_peers = [at((x + k) % 4, y, c, z) for k in range(1, 4)]
    plane = [{"op": (op + k) % 32, "sec": z} for k in range(1, 32)]
    twin = at(x, y, 1 - c, z)

    barrier = pltpu.get_barrier_semaphore()
    for peer in z_peers + plane:
        pl.semaphore_signal(barrier, inc=1, device_id=peer, device_id_type=MESH)

    stages, marks = plan
    mine = xb1.at[x, y, c, z // 4, pl.ds(pl.multiple_of((z % 4) * 32, 32), 32)]
    loads = [
        pltpu.make_async_copy(w_ref, mine, local_sem.at[0]),
        pltpu.make_async_copy(right_hbm, right, local_sem.at[1]),
        pltpu.make_async_copy(left_hbm, left, local_sem.at[2]),
        pltpu.make_async_copy(basis_hbm, basis, local_sem.at[3]),
    ]
    for load in loads:
        load.start()
    half[0] = jnp.zeros((128, 128), BF)
    sums[CHUNKS] = jnp.zeros((128, 128), F32)
    loads[0].wait()
    pl.semaphore_wait(barrier, 38)

    copies = []

    def push(src, to):
        i = len(copies)
        copy = remote(src, src, ag_send.at[i], ag_recv.at[i], to)
        copy.start()
        copies.append(copy)
        return copy

    along_z = [push(mine, z_peers[k]) for k in (3, 2, 4, 1, 5, 0, 6)]

    *tables, over = sort_terms(
        tl_ref[...], tr_ref[...], ts_ref[...], tt_ref[...], count_ref[0], x, y, plan
    )
    for i, table in enumerate(tables):
        tab_v[i] = table
    to_smem = pltpu.make_async_copy(tab_v, tab_s, local_sem.at[4])
    to_smem.start()

    def even(buf, dx, dy):
        return buf.at[(x + dx) % 4, (y + dy) % 4, c, 0]

    def odd(buf, dx, dy):
        return buf.at[(x + dx) % 4, (y + dy) % 4, c, 1]

    relays = []

    def relay(view):
        relays.append(push(view, twin))

    def push_to(src, dst, to):
        i = len(copies)
        copy = remote(src, dst, ag_send.at[i], ag_recv.at[i], to)
        copy.start()
        copies.append(copy)
        return copy

    def spread_even(d):
        dst = even(xb2 if d else xb1, 0, d)
        src = even(xb1, 0, d)
        return push_to(src, dst, x_peers[0]), push_to(src, dst, x_peers[2])

    def spread_odd(d):
        dst = odd(xb2 if d else xb1, d, 0)
        src = odd(xb1, d, 0)
        return push_to(src, dst, y_peers[0]), push_to(src, dst, y_peers[2])

    def forward_even(d, pair):
        buf = xb2 if d else xb1
        for copy in pair:
            copy.wait_recv()
        relay(even(buf, 3, d))
        relay(even(buf, 1, d))
        step = jnp.where((y + d) % 2 == 0, 3, 1)
        return push_to(even(buf, step, d), even(xb3, step, d), at((x + 4 - step) % 4, y, c, z))

    def forward_odd(d, pair):
        buf = xb2 if d else xb1
        for copy in pair:
            copy.wait_recv()
        relay(odd(buf, d, 3))
        relay(odd(buf, d, 1))
        step = jnp.where((x + d) % 2 == 0, 3, 1)
        return push_to(odd(buf, d, step), odd(xb3, d, step), at(x, (y + 4 - step) % 4, c, z))

    for copy in along_z:
        copy.wait_recv()
    y_even = {k: push(even(xb1, 0, 0), y_peers[k - 1]) for k in (1, 3)}
    x_odd = {k: push(odd(xb1, 0, 0), x_peers[k - 1]) for k in (1, 3)}
    evens, odds = {0: spread_even(0)}, {0: spread_odd(0)}
    y_even[2] = push(even(xb1, 0, 0), y_peers[1])
    x_odd[2] = push(odd(xb1, 0, 0), x_peers[1])
    relay(xb1.at[x, y, c])
    for k in (1, 3):
        y_even[k].wait_recv()
        evens[4 - k] = spread_even(4 - k)
        relay(even(xb1, 0, 4 - k))
        x_odd[k].wait_recv()
        odds[4 - k] = spread_odd(4 - k)
        relay(odd(xb1, 4 - k, 0))
    farthest = {0: (forward_even(0, evens[0]), forward_odd(0, odds[0]))}
    y_even[2].wait_recv()
    evens[2] = spread_even(2)
    relay(even(xb1, 0, 2))
    x_odd[2].wait_recv()
    odds[2] = spread_odd(2)
    relay(odd(xb1, 2, 0))
    to_smem.wait()
    for load in loads[1:]:
        load.wait()

    def products(first, count, steps, buf):
        unroll = count // steps

        def step(i, carry):
            for u in range(unroll):
                slot = first + i * unroll + u
                word = tab_s[0, slot >> 7, slot & 127]
                l, s = word & 63, word >> 6
                block = buf[s >> 4, (s >> 2) & 3, (s >> 1) & 1, s & 1]
                half[slot + 1] = jnp.dot(left[l], block, preferred_element_type=F32).astype(BF)
            return carry

        if count:
            lax.fori_loop(0, steps, step, 0)

    def relayed():
        for copy in relays:
            copy.wait_recv()
        relays.clear()

    kept = []

    def keep_on(src, dst, parts):
        for part_of in parts:
            copy = pltpu.make_async_copy(
                part_of(src), part_of(dst), local_sem.at[5 + len(kept)]
            )
            copy.start()
            kept.append(copy)

    crossing = [lambda b: b.at[x, :, :, 0], lambda b: b.at[:, y, :, 1]]
    beside = [lambda b, d=d: b.at[(x + d) % 4, y, :, 0] for d in (1, 3)]
    beside += [lambda b, d=d: b.at[x, (y + d) % 4, :, 1] for d in (1, 3)]
    flanks = [lambda b, d=d: b.at[(x + d) % 4, :, :, 0] for d in (1, 3)]
    flanks += [lambda b, d=d: b.at[:, (y + d) % 4, :, 1] for d in (1, 3)]

    relayed()
    keep_on(xb1, xb2, crossing + beside)
    products(0, stages[0], 2, xb1)
    for d in (3, 1, 2):
        farthest[d] = (forward_even(d, evens[d]), forward_odd(d, odds[d]))
    relayed()
    for copy in kept:
        copy.wait()
    keep_on(xb2, xb3, crossing + flanks)
    early = stages[1] * 9 // 13 // 8 * 8
    products(stages[0], early, 2, xb2)
    for d in (0, 3, 1, 2):
        for copy in farthest[d]:
            copy.wait_recv()
        relay(even(xb3, 2, d))
        relay(odd(xb3, d, 2))
    products(stages[0] + early, stages[1] - early, 1, xb2)
    relayed()
    for copy in kept[6:]:
        copy.wait()
    products(stages[0] + stages[1], stages[2], 8 if stages[2] > 512 else 2, xb3)

    def chunk_sums(first, unroll, i, acc):
        for v in range(unroll):
            chunk = first + i * unroll + v
            words = []
            for k in range(CHUNK):
                slot = chunk * CHUNK + k
                words.append(tab_s[1 + (slot >> 10), (slot >> 7) & 7, slot & 127])
            halves = jnp.concatenate([half[w & 2047] for w in words], axis=1)
            rights = jnp.concatenate([right[w >> 11] for w in words], axis=1)
            prod = lax.dot_general(halves, rights, NT, preferred_element_type=F32)
            keep = tab_s[3, chunk >> 7, chunk & 127]
            acc = acc * keep.astype(F32) + prod
            sums[chunk] = acc
        return acc

    def send_parts(p):
        for h in range(2):
            total = sums[tab_s[3, 2, 2 * p + h]]
            sig[2 * p + h] = total
            part[p, 4 * h : 4 * h + 4] = total.astype(BF).reshape(4, 32, 128)
        for k in range(8):
            xo, co = (x + k // 2) % 4, (c + k) % 2
            yo = (p - xo + 4) % 4
            owner = (xo * 4 + yo) * 2 + co
            index = (op - owner + 31) % 32
            copy = remote(
                part.at[p, xo * 2 + co],
                inbox.at[index],
                rs_send,
                rs_recv,
                {"op": owner, "sec": z},
            )
            if k == 0:
                pl.when(owner != op)(copy.start)
            else:
                copy.start()

    p_me, m_me = (x + y) % 4, x * 2 + c
    t_me, r_me = 2 * p_me + m_me // 4, pl.multiple_of((m_me % 4) * 32, 32)
    out_mine = outbox.at[t_me, pl.ds(r_me, 32)]
    whole = remote(inbox, inbox, rs_send, rs_recv, twin)
    to_out = [
        remote(out_mine, out_mine, out_send.at[k], out_recv.at[k], peer)
        for k, peer in enumerate(plane)
    ]

    def send_sum():
        whole.wait_recv()
        total = part[p_me, m_me].astype(F32)
        for k in range(31):
            total = total + inbox[k].astype(F32)
        out_mine[...] = total.astype(BF)
        for copy in to_out:
            copy.start()

    def inner(p, sums_k):
        new = []
        for k in range(4):
            acc = sums_k[k]
            for b in (2 * p, 2 * p + 1):
                prod = basis[k, b].astype(F32) * sig[b]
                acc = acc + jnp.sum(prod.reshape(16, 8, 128), axis=0)
            new.append(acc)
        return new

    acc = jnp.zeros((128, 128), F32)
    dots = [jnp.zeros((8, 128), F32) for _ in range(4)]
    for p in range(4):
        first = marks[p - 1] if p else 0
        count = marks[p] - first
        if count:
            steps = 8 if count > 64 else 2
            acc = lax.fori_loop(
                0, steps, functools.partial(chunk_sums, first, count // steps), acc
            )
        send_parts(p)
        dots = inner(p, dots)
        if p >= 2:
            pl.when(p_me == p - 2)(send_sum)

    lane = lax.broadcasted_iota(I32, (1, 128), 1)
    line = jnp.where(lane == 4, over.astype(F32), 0.0)
    for k in range(4):
        total = jnp.sum(jnp.sum(dots[k], axis=0, keepdims=True), axis=1, keepdims=True)
        line = line + jnp.where(lane == k, total, 0.0)
    corr_z[z] = line
    to_z = []
    for k, peer in enumerate(z_peers):
        copy = remote(corr_z.at[z], corr_z.at[z], cz_send.at[k], cz_recv.at[k], peer)
        copy.start()
        to_z.append(copy)

    pl.when(p_me == 2)(send_sum)
    pl.when(p_me == 3)(send_sum)

    for copy in to_z:
        copy.wait_recv()
    z_sum = corr_z[0]
    for k in range(1, 8):
        z_sum = z_sum + corr_z[k]
    corr_p[op] = z_sum
    to_plane = []
    for k, peer in enumerate(plane):
        copy = remote(corr_p.at[op], corr_p.at[op], cp_send.at[k], cp_recv.at[k], peer)
        copy.start()
        to_plane.append(copy)

    for copy in to_out:
        copy.wait_recv()
    sigma_ref[...] = outbox[...].astype(F32)
    for copy in to_plane:
        copy.wait_recv()
    p_sum = corr_p[0]
    for k in range(1, 32):
        p_sum = p_sum + corr_p[k]
    for k in range(4):
        corr_ref[k] = jnp.sum(jnp.where(lane == k, p_sum, 0.0))
    over_ref[0] = jnp.sum(jnp.where(lane == 4, p_sum, 0.0))

    for copy in copies + to_z + to_out + to_plane:
        copy.wait_send()
    whole.wait_send()


def run(plan, which, arrays):
    vmem = pl.BlockSpec(memory_space=pltpu.VMEM)
    smem = pl.BlockSpec(memory_space=pltpu.SMEM)
    hbm = pl.BlockSpec(memory_space=pltpu.HBM)
    dma = pltpu.SemaphoreType.DMA
    return pl.pallas_call(
        functools.partial(kernel, plan),
        out_shape=(
            jax.ShapeDtypeStruct((8, 128, 128), F32),
            jax.ShapeDtypeStruct((4,), F32),
            jax.ShapeDtypeStruct((1,), F32),
        ),
        in_specs=[vmem, hbm, hbm, hbm, vmem, vmem, vmem, vmem, smem],
        out_specs=(vmem, smem, smem),
        scratch_shapes=[
            pltpu.VMEM((4, 4, 2, 2, 128, 128), BF),
            pltpu.VMEM((4, 4, 2, 2, 128, 128), BF),
            pltpu.VMEM((4, 4, 2, 2, 128, 128), BF),
            pltpu.VMEM((64, 128, 128), BF),
            pltpu.VMEM((64, 128, 128), BF),
            pltpu.VMEM((4, 8, 128, 128), BF),
            pltpu.VMEM((SLOTS + 1, 128, 128), BF),
            pltpu.VMEM((CHUNKS + 1, 128, 128), F32),
            pltpu.VMEM((4, 8, 128), I32),
            pltpu.SMEM((4, 8, 128), I32),
            pltpu.VMEM((8, 128, 128), F32),
            pltpu.VMEM((4, 8, 32, 128), BF),
            pltpu.VMEM((31, 32, 128), BF),
            pltpu.VMEM((8, 128, 128), BF),
            pltpu.VMEM((8, 1, 128), F32),
            pltpu.VMEM((32, 1, 128), F32),
            dma((17,)),
            dma((80,)),
            dma((80,)),
            dma(()),
            dma(()),
            dma((31,)),
            dma((31,)),
            dma((7,)),
            dma((7,)),
            dma((31,)),
            dma((31,)),
        ],
        compiler_params=pltpu.CompilerParams(
            collective_id=which, has_side_effects=True, vmem_limit_bytes=60 * 1024 * 1024
        ),
    )(*arrays)


def body(wavefunction, left_ops, right_ops, basis, tl, tr, ts, tt, count):
    terms = (t.reshape(8, 128) for t in (tl, tr, ts, tt))
    arrays = (wavefunction, left_ops, right_ops, basis, *terms, count)
    sigma, corr, over = run(STAGED, 0, arrays)
    return lax.cond(
        over[0] > 0, lambda: tuple(run(GENERAL, 1, arrays)[:2]), lambda: (sigma, corr)
    )


def solution(mesh):
    placed = (
        P(("op", "sec"), None),
        P(("op", "sec"), None, None),
        P(("op", "sec"), None, None),
        P(None, "sec", None, None),
        P(("op", "sec")),
        P(("op", "sec")),
        P(("op", "sec")),
        P(("op", "sec")),
        P(("op", "sec")),
    )
    return jax.shard_map(
        body, mesh=mesh, in_specs=placed, out_specs=(P("sec", None, None), P()), check_vma=False
    )
```

```python
import functools

import jax
import jax.numpy as jnp
from jax import lax
from jax.experimental import pallas as pl
from jax.experimental.pallas import tpu as pltpu
from jax.sharding import PartitionSpec as P

MESH = pl.DeviceIdType.MESH
BF, F32, I32 = jnp.bfloat16, jnp.float32, jnp.int32
SLOTS = 1024
CHUNK = 8
CHUNKS = 136
STAGED = ((304, 392, 328), (44, 78, 108, 136))
GENERAL = ((0, 0, 1024), (136, 136, 136, 136))
NT = (((1,), (1,)), ((), ()))


def remote(src, dst, send_sem, recv_sem, to):
    return pltpu.make_async_remote_copy(
        src_ref=src,
        dst_ref=dst,
        send_sem=send_sem,
        recv_sem=recv_sem,
        device_id=to,
        device_id_type=MESH,
    )


def fold(mask_or_value):
    return jnp.sum(mask_or_value.reshape(16, 8, 128), axis=0)


def ranks_of(key):
    key_t = key.T
    ranks = [jnp.zeros((8, 128), I32) for _ in range(8)]
    for j in range(8):
        key_j = jnp.broadcast_to(key_t[:, j : j + 1], (128, 128))
        for i in range(8):
            ranks[i] = ranks[i] + fold((key_j < key[i : i + 1, :]).astype(I32))
    return jnp.concatenate([jnp.sum(r, axis=0, keepdims=True) for r in ranks], axis=0)


def scatter(place, value, rows):
    place_t, value_t = place.T, value.T
    tables = [jnp.zeros((8, 128), I32) for _ in range(rows)]
    for j in range(8):
        place_j = jnp.broadcast_to(place_t[:, j : j + 1], (128, 128))
        value_j = jnp.broadcast_to(value_t[:, j : j + 1], (128, 128))
        for i in range(rows):
            at = lax.broadcasted_iota(I32, (128, 128), 1) + i * 128
            tables[i] = tables[i] + fold(jnp.where(place_j == at, value_j, 0))
    return [jnp.sum(t, axis=0, keepdims=True) for t in tables]


def count_of(mask):
    return jnp.sum(jnp.sum(mask.astype(I32), axis=0, keepdims=True), axis=1, keepdims=True)


def sort_terms(tl, tr, ts, tt, count, x, y, plan):
    row = lax.broadcasted_iota(I32, (8, 128), 0)
    lane = lax.broadcasted_iota(I32, (8, 128), 1)
    slot = row * 128 + lane
    live = slot < count

    dx, dy, odd = ((ts >> 4) - x) & 3, ((ts >> 2) - y) & 3, (ts & 1) == 1
    near, far = jnp.where(odd, dx, dy), jnp.where(odd, dy, dx)
    late = jnp.where((far == 0) | (near == 0), 0, 1)
    late = jnp.where(far == 2, 2, late)
    stages, marks = plan
    spot = ranks_of(jnp.where(live, late, 3) * SLOTS + slot)
    done, end = jnp.zeros((1, 1), I32), jnp.zeros((1, 1), I32)
    for i in range(3):
        n = count_of(live & (late == i))
        begin = jnp.maximum(end, sum(stages[:i]))
        spot = spot + jnp.where(late == i, begin - done, 0)
        done, end = done + n, begin + n
    over = jnp.maximum(end - SLOTS, 0)
    spot = jnp.where(live, spot, 1 << 20)
    first = jnp.concatenate(scatter(spot, tl | (ts << 6), 8), axis=0)
    spot = jnp.minimum(spot, SLOTS - 1)

    rank = ranks_of(jnp.where(live, tt, 8) * SLOTS + slot)
    base = jnp.zeros((1, 1), I32)
    start = jnp.zeros((1, 1), I32)
    place = jnp.where(live, rank, 1 << 20)
    restart = jnp.zeros((8, 128), I32)
    last = jnp.full((8, 128), CHUNKS, I32)
    for t in range(8):
        hit = live & (tt == t)
        n = count_of(hit)
        place = place + jnp.where(hit, start - base, 0)
        restart = restart | ((start == slot * CHUNK) & (n > 0)).astype(I32)
        base = base + n
        start = start + (((n + CHUNK - 1) >> 3) << 3)
        last = jnp.where((lane == t) & (n > 0), (start >> 3) - 1, last)
        over = jnp.maximum(over, start - CHUNK * marks[t // 2])
    tables = scatter(place, (spot + 1) | (tr << 11), 9)
    tail = jnp.concatenate([tables[8], jnp.zeros((7, 128), I32)], axis=0)
    ends = jnp.where(row < 2, 1 - restart, last)
    return first, jnp.concatenate(tables[:8], axis=0), tail, ends, over


def kernel(
    plan,
    w_ref,
    left_hbm,
    right_hbm,
    basis_hbm,
    tl_ref,
    tr_ref,
    ts_ref,
    tt_ref,
    count_ref,
    sigma_ref,
    corr_ref,
    over_ref,
    xb1,
    xb2,
    xb3,
    left,
    right,
    basis,
    half,
    sums,
    tab_v,
    tab_s,
    sig,
    part,
    inbox,
    outbox,
    corr_z,
    corr_p,
    local_sem,
    relay_send,
    relay_recv,
    ag_send,
    ag_recv,
    rs_send,
    rs_recv,
    out_send,
    out_recv,
    cz_send,
    cz_recv,
    cp_send,
    cp_recv,
):
    op = lax.axis_index("op")
    z = lax.axis_index("sec")
    x, y, c = op // 8, (op // 2) % 4, op % 2

    def at(xx, yy, cc, zz):
        return {"op": (xx * 4 + yy) * 2 + cc, "sec": zz}

    z_peers = [at(x, y, c, (z + k) % 8) for k in range(1, 8)]
    y_peers = [at(x, (y + k) % 4, c, z) for k in range(1, 4)]
    x_peers = [at((x + k) % 4, y, c, z) for k in range(1, 4)]
    plane = [{"op": (op + k) % 32, "sec": z} for k in range(1, 32)]
    twin = at(x, y, 1 - c, z)

    barrier = pltpu.get_barrier_semaphore()
    for peer in z_peers + plane:
        pl.semaphore_signal(barrier, inc=1, device_id=peer, device_id_type=MESH)

    stages, marks = plan
    mine = xb1.at[x, y, c, z // 4, pl.ds(pl.multiple_of((z % 4) * 32, 32), 32)]
    loads = [
        pltpu.make_async_copy(w_ref, mine, local_sem.at[0]),
        pltpu.make_async_copy(right_hbm, right, local_sem.at[1]),
        pltpu.make_async_copy(left_hbm, left, local_sem.at[2]),
        pltpu.make_async_copy(basis_hbm, basis, local_sem.at[3]),
    ]
    for load in loads:
        load.start()
    half[0] = jnp.zeros((128, 128), BF)
    sums[CHUNKS] = jnp.zeros((128, 128), F32)
    loads[0].wait()
    pl.semaphore_wait(barrier, 38)

    copies = []

    def push(src, to):
        i = len(copies)
        copy = remote(src, src, ag_send.at[i], ag_recv.at[i], to)
        copy.start()
        copies.append(copy)
        return copy

    along_z = [push(mine, z_peers[k]) for k in (3, 2, 4, 1, 5, 0, 6)]

    *tables, over = sort_terms(
        tl_ref[...], tr_ref[...], ts_ref[...], tt_ref[...], count_ref[0], x, y, plan
    )
    for i, table in enumerate(tables):
        tab_v[i] = table
    to_smem = pltpu.make_async_copy(tab_v, tab_s, local_sem.at[4])
    to_smem.start()

    def even(buf, dx, dy):
        return buf.at[(x + dx) % 4, (y + dy) % 4, c, 0]

    def odd(buf, dx, dy):
        return buf.at[(x + dx) % 4, (y + dy) % 4, c, 1]

    def relay(view, stage):
        remote(view, view, relay_send, relay_recv.at[stage], twin).start()

    def push_to(src, dst, to):
        i = len(copies)
        copy = remote(src, dst, ag_send.at[i], ag_recv.at[i], to)
        copy.start()
        copies.append(copy)
        return copy

    def spread_even(d):
        dst = even(xb2 if d else xb1, 0, d)
        src = even(xb1, 0, d)
        return push_to(src, dst, x_peers[0]), push_to(src, dst, x_peers[2])

    def spread_odd(d):
        dst = odd(xb2 if d else xb1, d, 0)
        src = odd(xb1, d, 0)
        return push_to(src, dst, y_peers[0]), push_to(src, dst, y_peers[2])

    def forward_even(d, pair):
        buf = xb2 if d else xb1
        for copy in pair:
            copy.wait_recv()
        relay(even(buf, 3, d), 1 if d else 0)
        relay(even(buf, 1, d), 1 if d else 0)
        step = jnp.where((y + d) % 2 == 0, 3, 1)
        return push_to(even(buf, step, d), even(xb3, step, d), at((x + 4 - step) % 4, y, c, z))

    def forward_odd(d, pair):
        buf = xb2 if d else xb1
        for copy in pair:
            copy.wait_recv()
        relay(odd(buf, d, 3), 1 if d else 0)
        relay(odd(buf, d, 1), 1 if d else 0)
        step = jnp.where((x + d) % 2 == 0, 3, 1)
        return push_to(odd(buf, d, step), odd(xb3, d, step), at(x, (y + 4 - step) % 4, c, z))

    for copy in along_z:
        copy.wait_recv()
    y_even = {k: push(even(xb1, 0, 0), y_peers[k - 1]) for k in (1, 3)}
    x_odd = {k: push(odd(xb1, 0, 0), x_peers[k - 1]) for k in (1, 3)}
    evens, odds = {0: spread_even(0)}, {0: spread_odd(0)}
    y_even[2] = push(even(xb1, 0, 0), y_peers[1])
    x_odd[2] = push(odd(xb1, 0, 0), x_peers[1])
    relay(xb1.at[x, y, c], 0)
    for k in (1, 3):
        y_even[k].wait_recv()
        evens[4 - k] = spread_even(4 - k)
        relay(even(xb1, 0, 4 - k), 0)
        x_odd[k].wait_recv()
        odds[4 - k] = spread_odd(4 - k)
        relay(odd(xb1, 4 - k, 0), 0)
    farthest = {0: (forward_even(0, evens[0]), forward_odd(0, odds[0]))}
    y_even[2].wait_recv()
    evens[2] = spread_even(2)
    relay(even(xb1, 0, 2), 0)
    x_odd[2].wait_recv()
    odds[2] = spread_odd(2)
    relay(odd(xb1, 2, 0), 0)
    to_smem.wait()
    for load in loads[1:]:
        load.wait()

    def products(first, count, steps, buf):
        unroll = count // steps

        def step(i, carry):
            for u in range(unroll):
                slot = first + i * unroll + u
                word = tab_s[0, slot >> 7, slot & 127]
                l, s = word & 63, word >> 6
                block = buf[s >> 4, (s >> 2) & 3, (s >> 1) & 1, s & 1]
                half[slot + 1] = jnp.dot(left[l], block, preferred_element_type=F32).astype(BF)
            return carry

        if count:
            lax.fori_loop(0, steps, step, 0)

    sizes = (xb1.at[0, pl.ds(0, 3)], xb2.at[0, pl.ds(0, 3)], xb3.at[0, pl.ds(0, 2)])

    def relayed(stage):
        view = sizes[stage]
        remote(view, view, relay_send, relay_recv.at[stage], twin).wait_recv()

    kept = []

    def keep_on(src, dst, parts):
        for part_of in parts:
            copy = pltpu.make_async_copy(
                part_of(src), part_of(dst), local_sem.at[5 + len(kept)]
            )
            copy.start()
            kept.append(copy)

    crossing = [lambda b: b.at[x, :, :, 0], lambda b: b.at[:, y, :, 1]]
    beside = [lambda b, d=d: b.at[(x + d) % 4, y, :, 0] for d in (1, 3)]
    beside += [lambda b, d=d: b.at[x, (y + d) % 4, :, 1] for d in (1, 3)]
    flanks = [lambda b, d=d: b.at[(x + d) % 4, :, :, 0] for d in (1, 3)]
    flanks += [lambda b, d=d: b.at[:, (y + d) % 4, :, 1] for d in (1, 3)]

    relayed(0)
    keep_on(xb1, xb2, crossing + beside)
    products(0, stages[0], 2, xb1)
    for d in (3, 1, 2):
        farthest[d] = (forward_even(d, evens[d]), forward_odd(d, odds[d]))
    relayed(1)
    for copy in kept:
        copy.wait()
    keep_on(xb2, xb3, crossing + flanks)
    early = stages[1] * 9 // 13 // 8 * 8
    products(stages[0], early, 2, xb2)
    for d in (0, 3, 1, 2):
        for copy in farthest[d]:
            copy.wait_recv()
        relay(even(xb3, 2, d), 2)
        relay(odd(xb3, d, 2), 2)
    products(stages[0] + early, stages[1] - early, 1, xb2)
    relayed(2)
    for copy in kept[6:]:
        copy.wait()
    products(stages[0] + stages[1], stages[2], 8 if stages[2] > 512 else 2, xb3)

    def chunk_sums(first, unroll, i, acc):
        for v in range(unroll):
            chunk = first + i * unroll + v
            words = []
            for k in range(CHUNK):
                slot = chunk * CHUNK + k
                words.append(tab_s[1 + (slot >> 10), (slot >> 7) & 7, slot & 127])
            halves = jnp.concatenate([half[w & 2047] for w in words], axis=1)
            rights = jnp.concatenate([right[w >> 11] for w in words], axis=1)
            prod = lax.dot_general(halves, rights, NT, preferred_element_type=F32)
            keep = tab_s[3, chunk >> 7, chunk & 127]
            acc = acc * keep.astype(F32) + prod
            sums[chunk] = acc
        return acc

    def send_parts(p):
        for h in range(2):
            total = sums[tab_s[3, 2, 2 * p + h]]
            sig[2 * p + h] = total
            part[p, 4 * h : 4 * h + 4] = total.astype(BF).reshape(4, 32, 128)
        for k in range(8):
            xo, co = (x + k // 2) % 4, (c + k) % 2
            yo = (p - xo + 4) % 4
            owner = (xo * 4 + yo) * 2 + co
            index = (op - owner + 31) % 32
            copy = remote(
                part.at[p, xo * 2 + co],
                inbox.at[index],
                rs_send,
                rs_recv,
                {"op": owner, "sec": z},
            )
            if k == 0:
                pl.when(owner != op)(copy.start)
            else:
                copy.start()

    p_me, m_me = (x + y) % 4, x * 2 + c
    t_me, r_me = 2 * p_me + m_me // 4, pl.multiple_of((m_me % 4) * 32, 32)
    out_mine = outbox.at[t_me, pl.ds(r_me, 32)]
    whole = remote(inbox, inbox, rs_send, rs_recv, twin)
    to_out = [
        remote(out_mine, out_mine, out_send, out_recv, peer)
        for peer in plane
    ]

    def send_sum():
        whole.wait_recv()
        total = part[p_me, m_me].astype(F32)
        for k in range(31):
            total = total + inbox[k].astype(F32)
        out_mine[...] = total.astype(BF)
        for copy in to_out:
            copy.start()

    def inner(b, dots):
        new = []
        for k in range(4):
            prod = basis[k, b].astype(F32) * sig[b]
            new.append(dots[k] + jnp.sum(prod.reshape(16, 8, 128), axis=0))
        return new

    def segment(first, unroll, ready, i, carry):
        acc, dots = carry[0], list(carry[1:])
        if ready is not None:
            dots = inner(2 * ready + i, dots)
        return (chunk_sums(first, unroll, i, acc), *dots)

    carry = (jnp.zeros((128, 128), F32), *(jnp.zeros((8, 128), F32) for _ in range(4)))
    for p in range(4):
        first = marks[p - 1] if p else 0
        count = marks[p] - first
        ready = p - 1 if p else None
        if count:
            steps = 8 if count > 64 else 2
            step = functools.partial(segment, first, count // steps, ready)
            carry = lax.fori_loop(0, steps, step, carry)
        elif p:
            dots = inner(2 * ready + 1, inner(2 * ready, list(carry[1:])))
            carry = (carry[0], *dots)
        send_parts(p)
    dots = inner(7, inner(6, list(carry[1:])))

    lane = lax.broadcasted_iota(I32, (1, 128), 1)
    line = jnp.where(lane == 4, over.astype(F32), 0.0)
    for k in range(4):
        total = jnp.sum(jnp.sum(dots[k], axis=0, keepdims=True), axis=1, keepdims=True)
        line = line + jnp.where(lane == k, total, 0.0)
    corr_z[z] = line
    for peer in z_peers:
        remote(corr_z.at[z], corr_z.at[z], cz_send, cz_recv, peer).start()

    pl.when(p_me == 0)(send_sum)
    pl.when(p_me == 1)(send_sum)
    for copy in copies:
        copy.wait_send()
    remote(xb1.at[pl.ds(0, 2)], xb1.at[pl.ds(0, 2)], relay_send, relay_recv.at[0], twin).wait_send()
    pl.when(p_me == 2)(send_sum)
    pl.when(p_me == 3)(send_sum)

    z_rows = corr_z.at[pl.ds(0, 7)]
    from_z = remote(z_rows, z_rows, cz_send, cz_recv, twin)
    from_z.wait_recv()
    z_sum = corr_z[0]
    for k in range(1, 8):
        z_sum = z_sum + corr_z[k]
    corr_p[op] = z_sum
    for peer in plane:
        remote(corr_p.at[op], corr_p.at[op], cp_send, cp_recv, peer).start()

    out_all = remote(inbox, inbox, out_send, out_recv, twin)
    out_all.wait_recv()
    sigma_ref[...] = outbox[...].astype(F32)
    p_rows = corr_p.at[pl.ds(0, 31)]
    from_plane = remote(p_rows, p_rows, cp_send, cp_recv, twin)
    from_plane.wait_recv()
    p_sum = corr_p[0]
    for k in range(1, 32):
        p_sum = p_sum + corr_p[k]
    for k in range(4):
        corr_ref[k] = jnp.sum(jnp.where(lane == k, p_sum, 0.0))
    over_ref[0] = jnp.sum(jnp.where(lane == 4, p_sum, 0.0))

    for copy in (whole, from_z, out_all, from_plane):
        copy.wait_send()


def run(plan, which, arrays):
    vmem = pl.BlockSpec(memory_space=pltpu.VMEM)
    smem = pl.BlockSpec(memory_space=pltpu.SMEM)
    hbm = pl.BlockSpec(memory_space=pltpu.HBM)
    dma = pltpu.SemaphoreType.DMA
    return pl.pallas_call(
        functools.partial(kernel, plan),
        out_shape=(
            jax.ShapeDtypeStruct((8, 128, 128), F32),
            jax.ShapeDtypeStruct((4,), F32),
            jax.ShapeDtypeStruct((1,), F32),
        ),
        in_specs=[vmem, hbm, hbm, hbm, vmem, vmem, vmem, vmem, smem],
        out_specs=(vmem, smem, smem),
        scratch_shapes=[
            pltpu.VMEM((4, 4, 2, 2, 128, 128), BF),
            pltpu.VMEM((4, 4, 2, 2, 128, 128), BF),
            pltpu.VMEM((4, 4, 2, 2, 128, 128), BF),
            pltpu.VMEM((64, 128, 128), BF),
            pltpu.VMEM((64, 128, 128), BF),
            pltpu.VMEM((4, 8, 128, 128), BF),
            pltpu.VMEM((SLOTS + 1, 128, 128), BF),
            pltpu.VMEM((CHUNKS + 1, 128, 128), F32),
            pltpu.VMEM((4, 8, 128), I32),
            pltpu.SMEM((4, 8, 128), I32),
            pltpu.VMEM((8, 128, 128), F32),
            pltpu.VMEM((4, 8, 32, 128), BF),
            pltpu.VMEM((31, 32, 128), BF),
            pltpu.VMEM((8, 128, 128), BF),
            pltpu.VMEM((8, 1, 128), F32),
            pltpu.VMEM((32, 1, 128), F32),
            dma((17,)),
            dma(()),
            dma((3,)),
            dma((80,)),
            dma((80,)),
            dma(()),
            dma(()),
            dma(()),
            dma(()),
            dma(()),
            dma(()),
            dma(()),
            dma(()),
        ],
        compiler_params=pltpu.CompilerParams(
            collective_id=which, has_side_effects=True, vmem_limit_bytes=63 * 1024 * 1024
        ),
    )(*arrays)


def body(wavefunction, left_ops, right_ops, basis, tl, tr, ts, tt, count):
    terms = (t.reshape(8, 128) for t in (tl, tr, ts, tt))
    arrays = (wavefunction, left_ops, right_ops, basis, *terms, count)
    sigma, corr, over = run(STAGED, 0, arrays)
    return lax.cond(
        over[0] > 0, lambda: tuple(run(GENERAL, 1, arrays)[:2]), lambda: (sigma, corr)
    )


def solution(mesh):
    placed = (
        P(("op", "sec"), None),
        P(("op", "sec"), None, None),
        P(("op", "sec"), None, None),
        P(None, "sec", None, None),
        P(("op", "sec")),
        P(("op", "sec")),
        P(("op", "sec")),
        P(("op", "sec")),
        P(("op", "sec")),
    )
    return jax.shard_map(
        body, mesh=mesh, in_specs=placed, out_specs=(P("sec", None, None), P()), check_vma=False
    )
```

```python
import functools

import jax
import jax.numpy as jnp
from jax import lax
from jax.experimental import pallas as pl
from jax.experimental.pallas import tpu as pltpu
from jax.sharding import PartitionSpec as P

MESH = pl.DeviceIdType.MESH
BF, F32, I32 = jnp.bfloat16, jnp.float32, jnp.int32
SLOTS = 1024
CHUNK = 8
CHUNKS = 136
STAGED = ((304, 392, 328), (44, 78, 108, 136))
GENERAL = ((0, 0, 1024), (136, 136, 136, 136))
NT = (((1,), (1,)), ((), ()))


def remote(src, dst, send_sem, recv_sem, to):
    return pltpu.make_async_remote_copy(
        src_ref=src,
        dst_ref=dst,
        send_sem=send_sem,
        recv_sem=recv_sem,
        device_id=to,
        device_id_type=MESH,
    )


def fold(mask_or_value):
    return jnp.sum(mask_or_value.reshape(16, 8, 128), axis=0)


def ranks_of(key):
    key_t = key.T
    ranks = [jnp.zeros((8, 128), I32) for _ in range(8)]
    for j in range(8):
        key_j = jnp.broadcast_to(key_t[:, j : j + 1], (128, 128))
        for i in range(8):
            ranks[i] = ranks[i] + fold((key_j < key[i : i + 1, :]).astype(I32))
    return jnp.concatenate([jnp.sum(r, axis=0, keepdims=True) for r in ranks], axis=0)


def scatter(place, value, rows):
    place_t, value_t = place.T, value.T
    tables = [jnp.zeros((8, 128), I32) for _ in range(rows)]
    for j in range(8):
        place_j = jnp.broadcast_to(place_t[:, j : j + 1], (128, 128))
        value_j = jnp.broadcast_to(value_t[:, j : j + 1], (128, 128))
        for i in range(rows):
            at = lax.broadcasted_iota(I32, (128, 128), 1) + i * 128
            tables[i] = tables[i] + fold(jnp.where(place_j == at, value_j, 0))
    return [jnp.sum(t, axis=0, keepdims=True) for t in tables]


def count_of(mask):
    return jnp.sum(jnp.sum(mask.astype(I32), axis=0, keepdims=True), axis=1, keepdims=True)


def sort_terms(tl, tr, ts, tt, count, x, y, plan):
    row = lax.broadcasted_iota(I32, (8, 128), 0)
    lane = lax.broadcasted_iota(I32, (8, 128), 1)
    slot = row * 128 + lane
    live = slot < count

    dx, dy, odd = ((ts >> 4) - x) & 3, ((ts >> 2) - y) & 3, (ts & 1) == 1
    near, far = jnp.where(odd, dx, dy), jnp.where(odd, dy, dx)
    late = jnp.where((far == 0) | (near == 0), 0, 1)
    late = jnp.where(far == 2, 2, late)
    stages, marks = plan
    spot = ranks_of(jnp.where(live, late, 3) * SLOTS + slot)
    done, end = jnp.zeros((1, 1), I32), jnp.zeros((1, 1), I32)
    for i in range(3):
        n = count_of(live & (late == i))
        begin = jnp.maximum(end, sum(stages[:i]))
        spot = spot + jnp.where(late == i, begin - done, 0)
        done, end = done + n, begin + n
    over = jnp.maximum(end - SLOTS, 0)
    spot = jnp.where(live, spot, 1 << 20)
    first = jnp.concatenate(scatter(spot, tl | (ts << 6), 8), axis=0)
    spot = jnp.minimum(spot, SLOTS - 1)

    rank = ranks_of(jnp.where(live, tt, 8) * SLOTS + slot)
    base = jnp.zeros((1, 1), I32)
    start = jnp.zeros((1, 1), I32)
    place = jnp.where(live, rank, 1 << 20)
    restart = jnp.zeros((8, 128), I32)
    last = jnp.full((8, 128), CHUNKS, I32)
    for t in range(8):
        hit = live & (tt == t)
        n = count_of(hit)
        place = place + jnp.where(hit, start - base, 0)
        restart = restart | ((start == slot * CHUNK) & (n > 0)).astype(I32)
        base = base + n
        start = start + (((n + CHUNK - 1) >> 3) << 3)
        last = jnp.where((lane == t) & (n > 0), (start >> 3) - 1, last)
        over = jnp.maximum(over, start - CHUNK * marks[t // 2])
    tables = scatter(place, (spot + 1) | (tr << 11), 9)
    tail = jnp.concatenate([tables[8], jnp.zeros((7, 128), I32)], axis=0)
    ends = jnp.where(row < 2, 1 - restart, last)
    return first, jnp.concatenate(tables[:8], axis=0), tail, ends, over


def kernel(
    plan,
    w_ref,
    left_hbm,
    right_hbm,
    basis_hbm,
    tl_ref,
    tr_ref,
    ts_ref,
    tt_ref,
    count_ref,
    sigma_ref,
    corr_ref,
    over_ref,
    xb1,
    xb2,
    xb3,
    left,
    right,
    basis,
    half,
    sums,
    tab_v,
    tab_s,
    sig,
    part,
    inbox,
    outbox,
    corr_z,
    corr_p,
    local_sem,
    relay_send,
    relay_recv,
    ag_send,
    ag_recv,
    rs_send,
    rs_recv,
    out_send,
    out_recv,
    cz_send,
    cz_recv,
    cp_send,
    cp_recv,
):
    op = lax.axis_index("op")
    z = lax.axis_index("sec")
    x, y, c = op // 8, (op // 2) % 4, op % 2

    def at(xx, yy, cc, zz):
        return {"op": (xx * 4 + yy) * 2 + cc, "sec": zz}

    z_peers = [at(x, y, c, (z + k) % 8) for k in range(1, 8)]
    y_peers = [at(x, (y + k) % 4, c, z) for k in range(1, 4)]
    x_peers = [at((x + k) % 4, y, c, z) for k in range(1, 4)]
    plane = [{"op": (op + k) % 32, "sec": z} for k in range(1, 32)]
    twin = at(x, y, 1 - c, z)

    barrier = pltpu.get_barrier_semaphore()
    for peer in z_peers + y_peers + x_peers + [twin]:
        pl.semaphore_signal(barrier, inc=1, device_id=peer, device_id_type=MESH)

    stages, marks = plan
    mine = xb1.at[x, y, c, z // 4, pl.ds(pl.multiple_of((z % 4) * 32, 32), 32)]
    loads = [
        pltpu.make_async_copy(w_ref, mine, local_sem.at[0]),
        pltpu.make_async_copy(right_hbm, right, local_sem.at[1]),
        pltpu.make_async_copy(left_hbm, left, local_sem.at[2]),
        pltpu.make_async_copy(basis_hbm, basis, local_sem.at[3]),
    ]
    for load in loads:
        load.start()
    half[0] = jnp.zeros((128, 128), BF)
    sums[CHUNKS] = jnp.zeros((128, 128), F32)
    loads[0].wait()
    pl.semaphore_wait(barrier, 14)

    copies = []

    def push(src, to):
        i = len(copies)
        copy = remote(src, src, ag_send.at[i], ag_recv.at[i], to)
        copy.start()
        copies.append(copy)
        return copy

    along_z = [push(mine, z_peers[k]) for k in (3, 2, 4, 1, 5, 0, 6)]

    *tables, over = sort_terms(
        tl_ref[...], tr_ref[...], ts_ref[...], tt_ref[...], count_ref[0], x, y, plan
    )
    for i, table in enumerate(tables):
        tab_v[i] = table
    to_smem = pltpu.make_async_copy(tab_v, tab_s, local_sem.at[4])
    to_smem.start()

    def even(buf, dx, dy):
        return buf.at[(x + dx) % 4, (y + dy) % 4, c, 0]

    def odd(buf, dx, dy):
        return buf.at[(x + dx) % 4, (y + dy) % 4, c, 1]

    def relay(view, stage):
        remote(view, view, relay_send, relay_recv.at[stage], twin).start()

    def push_to(src, dst, to):
        i = len(copies)
        copy = remote(src, dst, ag_send.at[i], ag_recv.at[i], to)
        copy.start()
        copies.append(copy)
        return copy

    def spread_even(d):
        dst = even(xb2 if d else xb1, 0, d)
        src = even(xb1, 0, d)
        return push_to(src, dst, x_peers[0]), push_to(src, dst, x_peers[2])

    def spread_odd(d):
        dst = odd(xb2 if d else xb1, d, 0)
        src = odd(xb1, d, 0)
        return push_to(src, dst, y_peers[0]), push_to(src, dst, y_peers[2])

    def forward_even(d, pair):
        buf = xb2 if d else xb1
        for copy in pair:
            copy.wait_recv()
        relay(even(buf, 3, d), 1 if d else 0)
        relay(even(buf, 1, d), 1 if d else 0)
        step = jnp.where((y + d) % 2 == 0, 3, 1)
        return push_to(even(buf, step, d), even(xb3, step, d), at((x + 4 - step) % 4, y, c, z))

    def forward_odd(d, pair):
        buf = xb2 if d else xb1
        for copy in pair:
            copy.wait_recv()
        relay(odd(buf, d, 3), 1 if d else 0)
        relay(odd(buf, d, 1), 1 if d else 0)
        step = jnp.where((x + d) % 2 == 0, 3, 1)
        return push_to(odd(buf, d, step), odd(xb3, d, step), at(x, (y + 4 - step) % 4, c, z))

    for copy in along_z:
        copy.wait_recv()
    y_even = {k: push(even(xb1, 0, 0), y_peers[k - 1]) for k in (1, 3)}
    x_odd = {k: push(odd(xb1, 0, 0), x_peers[k - 1]) for k in (1, 3)}
    evens, odds = {0: spread_even(0)}, {0: spread_odd(0)}
    y_even[2] = push(even(xb1, 0, 0), y_peers[1])
    x_odd[2] = push(odd(xb1, 0, 0), x_peers[1])
    relay(xb1.at[x, y, c], 0)
    for k in (1, 3):
        y_even[k].wait_recv()
        evens[4 - k] = spread_even(4 - k)
        relay(even(xb1, 0, 4 - k), 0)
        x_odd[k].wait_recv()
        odds[4 - k] = spread_odd(4 - k)
        relay(odd(xb1, 4 - k, 0), 0)
    farthest = {0: (forward_even(0, evens[0]), forward_odd(0, odds[0]))}
    y_even[2].wait_recv()
    evens[2] = spread_even(2)
    relay(even(xb1, 0, 2), 0)
    x_odd[2].wait_recv()
    odds[2] = spread_odd(2)
    relay(odd(xb1, 2, 0), 0)
    to_smem.wait()
    for load in loads[1:]:
        load.wait()

    def products(first, count, steps, buf):
        unroll = count // steps

        def step(i, carry):
            for u in range(unroll):
                slot = first + i * unroll + u
                word = tab_s[0, slot >> 7, slot & 127]
                l, s = word & 63, word >> 6
                block = buf[s >> 4, (s >> 2) & 3, (s >> 1) & 1, s & 1]
                half[slot + 1] = jnp.dot(left[l], block, preferred_element_type=F32).astype(BF)
            return carry

        if count:
            lax.fori_loop(0, steps, step, 0)

    sizes = (xb1.at[0, pl.ds(0, 3)], xb2.at[0, pl.ds(0, 3)], xb3.at[0, pl.ds(0, 2)])

    def relayed(stage):
        view = sizes[stage]
        remote(view, view, relay_send, relay_recv.at[stage], twin).wait_recv()

    kept = []

    def keep_on(src, dst, parts):
        for part_of in parts:
            copy = pltpu.make_async_copy(
                part_of(src), part_of(dst), local_sem.at[5 + len(kept)]
            )
            copy.start()
            kept.append(copy)

    crossing = [lambda b: b.at[x, :, :, 0], lambda b: b.at[:, y, :, 1]]
    beside = [lambda b, d=d: b.at[(x + d) % 4, y, :, 0] for d in (1, 3)]
    beside += [lambda b, d=d: b.at[x, (y + d) % 4, :, 1] for d in (1, 3)]
    flanks = [lambda b, d=d: b.at[(x + d) % 4, :, :, 0] for d in (1, 3)]
    flanks += [lambda b, d=d: b.at[:, (y + d) % 4, :, 1] for d in (1, 3)]

    relayed(0)
    keep_on(xb1, xb2, crossing + beside)
    products(0, stages[0], 2, xb1)
    for d in (3, 1, 2):
        farthest[d] = (forward_even(d, evens[d]), forward_odd(d, odds[d]))
    relayed(1)
    for copy in kept:
        copy.wait()
    keep_on(xb2, xb3, crossing + flanks)
    early = stages[1] * 9 // 13 // 8 * 8
    products(stages[0], early, 2, xb2)
    for d in (0, 3, 1, 2):
        for copy in farthest[d]:
            copy.wait_recv()
        relay(even(xb3, 2, d), 2)
        relay(odd(xb3, d, 2), 2)
    products(stages[0] + early, stages[1] - early, 1, xb2)
    relayed(2)
    for copy in kept[6:]:
        copy.wait()
    products(stages[0] + stages[1], stages[2], 8 if stages[2] > 512 else 2, xb3)

    def chunk_sums(first, unroll, i, acc):
        for v in range(unroll):
            chunk = first + i * unroll + v
            words = []
            for k in range(CHUNK):
                slot = chunk * CHUNK + k
                words.append(tab_s[1 + (slot >> 10), (slot >> 7) & 7, slot & 127])
            halves = jnp.concatenate([half[w & 2047] for w in words], axis=1)
            rights = jnp.concatenate([right[w >> 11] for w in words], axis=1)
            prod = lax.dot_general(halves, rights, NT, preferred_element_type=F32)
            keep = tab_s[3, chunk >> 7, chunk & 127]
            acc = acc * keep.astype(F32) + prod
            sums[chunk] = acc
        return acc

    def send_parts(p):
        for h in range(2):
            total = sums[tab_s[3, 2, 2 * p + h]]
            sig[2 * p + h] = total
            part[p, 4 * h : 4 * h + 4] = total.astype(BF).reshape(4, 32, 128)
        for k in range(8):
            xo, co = (x + k // 2) % 4, (c + k) % 2
            yo = (p - xo + 4) % 4
            owner = (xo * 4 + yo) * 2 + co
            index = (op - owner + 31) % 32
            copy = remote(
                part.at[p, xo * 2 + co],
                inbox.at[index],
                rs_send,
                rs_recv,
                {"op": owner, "sec": z},
            )
            if k == 0:
                pl.when(owner != op)(copy.start)
            else:
                copy.start()

    p_me, m_me = (x + y) % 4, x * 2 + c
    t_me, r_me = 2 * p_me + m_me // 4, pl.multiple_of((m_me % 4) * 32, 32)
    out_mine = outbox.at[t_me, pl.ds(r_me, 32)]
    whole = remote(inbox, inbox, rs_send, rs_recv, twin)
    to_out = [
        remote(out_mine, out_mine, out_send, out_recv, peer)
        for peer in plane
    ]

    def send_sum():
        whole.wait_recv()
        total = part[p_me, m_me].astype(F32)
        for k in range(31):
            total = total + inbox[k].astype(F32)
        out_mine[...] = total.astype(BF)
        for copy in to_out:
            copy.start()

    def inner(b, dots):
        new = []
        for k in range(4):
            prod = basis[k, b].astype(F32) * sig[b]
            new.append(dots[k] + jnp.sum(prod.reshape(16, 8, 128), axis=0))
        return new

    def segment(first, unroll, ready, i, carry):
        acc, dots = carry[0], list(carry[1:])
        if ready is not None:
            dots = inner(2 * ready + i, dots)
        return (chunk_sums(first, unroll, i, acc), *dots)

    carry = (jnp.zeros((128, 128), F32), *(jnp.zeros((8, 128), F32) for _ in range(4)))
    for p in range(4):
        first = marks[p - 1] if p else 0
        count = marks[p] - first
        ready = p - 1 if p else None
        if count:
            steps = 8 if count > 64 else 2
            step = functools.partial(segment, first, count // steps, ready)
            carry = lax.fori_loop(0, steps, step, carry)
        elif p:
            dots = inner(2 * ready + 1, inner(2 * ready, list(carry[1:])))
            carry = (carry[0], *dots)
        send_parts(p)
    dots = inner(7, inner(6, list(carry[1:])))

    lane = lax.broadcasted_iota(I32, (1, 128), 1)
    line = jnp.where(lane == 4, over.astype(F32), 0.0)
    for k in range(4):
        total = jnp.sum(jnp.sum(dots[k], axis=0, keepdims=True), axis=1, keepdims=True)
        line = line + jnp.where(lane == k, total, 0.0)
    corr_z[z] = line
    for peer in z_peers:
        remote(corr_z.at[z], corr_z.at[z], cz_send, cz_recv, peer).start()

    pl.when(p_me == 0)(send_sum)
    pl.when(p_me == 1)(send_sum)
    for copy in copies:
        copy.wait_send()
    remote(xb1.at[pl.ds(0, 2)], xb1.at[pl.ds(0, 2)], relay_send, relay_recv.at[0], twin).wait_send()
    pl.when(p_me == 2)(send_sum)
    pl.when(p_me == 3)(send_sum)

    z_rows = corr_z.at[pl.ds(0, 7)]
    from_z = remote(z_rows, z_rows, cz_send, cz_recv, twin)
    from_z.wait_recv()
    z_sum = corr_z[0]
    for k in range(1, 8):
        z_sum = z_sum + corr_z[k]
    corr_p[op] = z_sum
    for peer in plane:
        remote(corr_p.at[op], corr_p.at[op], cp_send, cp_recv, peer).start()

    out_all = remote(inbox, inbox, out_send, out_recv, twin)
    out_all.wait_recv()
    sigma_ref[...] = outbox[...].astype(F32)
    p_rows = corr_p.at[pl.ds(0, 31)]
    from_plane = remote(p_rows, p_rows, cp_send, cp_recv, twin)
    from_plane.wait_recv()
    p_sum = corr_p[0]
    for k in range(1, 32):
        p_sum = p_sum + corr_p[k]
    for k in range(4):
        corr_ref[k] = jnp.sum(jnp.where(lane == k, p_sum, 0.0))
    over_ref[0] = jnp.sum(jnp.where(lane == 4, p_sum, 0.0))

    for copy in (whole, from_z, out_all, from_plane):
        copy.wait_send()


def run(plan, which, arrays):
    vmem = pl.BlockSpec(memory_space=pltpu.VMEM)
    smem = pl.BlockSpec(memory_space=pltpu.SMEM)
    hbm = pl.BlockSpec(memory_space=pltpu.HBM)
    dma = pltpu.SemaphoreType.DMA
    return pl.pallas_call(
        functools.partial(kernel, plan),
        out_shape=(
            jax.ShapeDtypeStruct((8, 128, 128), F32),
            jax.ShapeDtypeStruct((4,), F32),
            jax.ShapeDtypeStruct((1,), F32),
        ),
        in_specs=[vmem, hbm, hbm, hbm, vmem, vmem, vmem, vmem, smem],
        out_specs=(vmem, smem, smem),
        scratch_shapes=[
            pltpu.VMEM((4, 4, 2, 2, 128, 128), BF),
            pltpu.VMEM((4, 4, 2, 2, 128, 128), BF),
            pltpu.VMEM((4, 4, 2, 2, 128, 128), BF),
            pltpu.VMEM((64, 128, 128), BF),
            pltpu.VMEM((64, 128, 128), BF),
            pltpu.VMEM((4, 8, 128, 128), BF),
            pltpu.VMEM((SLOTS + 1, 128, 128), BF),
            pltpu.VMEM((CHUNKS + 1, 128, 128), F32),
            pltpu.VMEM((4, 8, 128), I32),
            pltpu.SMEM((4, 8, 128), I32),
            pltpu.VMEM((8, 128, 128), F32),
            pltpu.VMEM((4, 8, 32, 128), BF),
            pltpu.VMEM((31, 32, 128), BF),
            pltpu.VMEM((8, 128, 128), BF),
            pltpu.VMEM((8, 1, 128), F32),
            pltpu.VMEM((32, 1, 128), F32),
            dma((17,)),
            dma(()),
            dma((3,)),
            dma((80,)),
            dma((80,)),
            dma(()),
            dma(()),
            dma(()),
            dma(()),
            dma(()),
            dma(()),
            dma(()),
            dma(()),
        ],
        compiler_params=pltpu.CompilerParams(
            collective_id=which, has_side_effects=True, vmem_limit_bytes=63 * 1024 * 1024
        ),
    )(*arrays)


def body(wavefunction, left_ops, right_ops, basis, tl, tr, ts, tt, count):
    terms = (t.reshape(8, 128) for t in (tl, tr, ts, tt))
    arrays = (wavefunction, left_ops, right_ops, basis, *terms, count)
    sigma, corr, over = run(STAGED, 0, arrays)
    return lax.cond(
        over[0] > 0, lambda: tuple(run(GENERAL, 1, arrays)[:2]), lambda: (sigma, corr)
    )


def solution(mesh):
    placed = (
        P(("op", "sec"), None),
        P(("op", "sec"), None, None),
        P(("op", "sec"), None, None),
        P(None, "sec", None, None),
        P(("op", "sec")),
        P(("op", "sec")),
        P(("op", "sec")),
        P(("op", "sec")),
        P(("op", "sec")),
    )
    return jax.shard_map(
        body, mesh=mesh, in_specs=placed, out_specs=(P("sec", None, None), P()), check_vma=False
    )
```
